256 devices in a mesh: ctx: 32 (over z, x_hi, core), ch: 8 (over y, x_lo).
Axes of the slice: x: 4 (x_hi: 2, x_lo: 2; x = x_hi * 2 + x_lo), y: 4, z: 8, core: 2. Of those that a mesh axis runs over, the one named last changes fastest.
Arguments:
- values: bfloat16 [2, 131072, 1024], P(None, 'ctx', 'ch'), may hold values from -6 to 6
- gate: bfloat16 [2, 131072, 1024], P(None, 'ctx', 'ch'), may hold values from -6 to 6
- cotangent: bfloat16 [2, 131072, 1024], P(None, 'ctx', 'ch'), may hold values from -1.1953125 to 1.1953125
- factor_one: bfloat16 [256, 512, 512], P('ctx', 'ch'), may hold values from -0.25 to 0.25
- factor_two: bfloat16 [512, 256, 256], P('ctx', 'ch'), may hold values from -0.375 to 0.375
Outputs:
- d_values: bfloat16 [2, 131072, 1024], P(None, 'ctx', 'ch')
- d_gate: bfloat16 [2, 131072, 1024], P(None, 'ctx', 'ch')
- grad_one: float32 [256, 512, 512], P('ctx', 'ch')
- grad_two: float32 [512, 256, 256], P('ctx', 'ch')
The draws below stay inside these ranges and needn't reach their ends.
All inputs are finite; a program needn't handle non-finite values.
Results may differ from the reference program's by a relative error of at most 0.015.
Values may be sent and summed in bfloat16 or wider, within the bound.
A program may use at most 64 MiB of HBM per device.

```python
import jax
import jax.numpy as jnp
from jax import lax

D = 1024
B1 = 256
B2 = 512
SEQS = 2
LEN = 131072
N_CH = 8


def levels(key, shape, cuts, low, top_value):
    factor_of, own = 1.0, jax.random.fold_in(key, 6)
    for position, parts in cuts:
        draws = jnp.exp(jax.random.uniform(jax.random.fold_in(own, position), (parts,), jnp.float32, low / len(cuts), top_value / len(cuts)))
        factor_of = factor_of * jnp.repeat(draws, shape[position] // parts).reshape([-1 if axis == position else 1 for axis in range(len(shape))])
    return factor_of


def centred(rng, extent, width, reach, split=(), dtype=jnp.bfloat16):
    factor_of = levels(rng, extent, split, -0.22, 0.18) if split else 1.0
    drawn = jax.random.normal(rng, extent, jnp.float32) * width * factor_of
    return jnp.minimum(jnp.maximum(drawn, -reach), reach).astype(dtype)


def setup_inputs(seed: int = 0) -> dict:
    seeds = jax.random.split(jax.random.key(seed), 6)
    values = centred(seeds[0], (SEQS, LEN, D), 1.0, 6.0, ((1, 32), (2, 8)))
    gate = centred(seeds[1], (SEQS, LEN, D), 1.0, 6.0, ((1, 32), (2, 8)))
    cotangent = centred(seeds[2], (SEQS, LEN, D), 0.2, 1.1953125, ((1, 32), (2, 8)))
    factor_one = centred(seeds[3], (B1, B2, B2), B2 ** -0.5, 0.25, ((0, 32), (1, 8)))
    factor_two = centred(seeds[4], (B2, B1, B1), B1 ** -0.5, 0.375, ((0, 32), (1, 8)))
    return dict(values=values, gate=gate, cotangent=cotangent, factor_one=factor_one, factor_two=factor_two)


def reference(values, gate, cotangent, factor_one, factor_two):
    group_width = D // N_CH
    gated = (values.astype(jnp.float32) * gate.astype(jnp.float32)).astype(jnp.bfloat16)
    inputs = gated.reshape(SEQS, B1, B2, D).transpose(1, 2, 0, 3)

    def forward_block(pair):
        weight, block = pair
        flat = block.reshape(B2, SEQS * D)
        return jnp.dot(weight, flat, preferred_element_type=jnp.float32).astype(jnp.bfloat16).reshape(B2, SEQS, D)

    mixed = lax.map(forward_block, (factor_one, inputs))
    upstream = cotangent.reshape(SEQS, B2, B1, D).transpose(1, 2, 0, 3)
    moved = mixed.transpose(1, 0, 2, 3)

    def backward_second(triple):
        weight, grads, block = triple
        flat = grads.reshape(B1, SEQS * D)
        back = jnp.dot(weight.T, flat, preferred_element_type=jnp.float32).astype(jnp.bfloat16).reshape(B1, SEQS, D)
        left = grads.astype(jnp.float32).reshape(B1, SEQS, N_CH, group_width)
        right = block.astype(jnp.float32).reshape(B1, SEQS, N_CH, group_width)
        partial_sums = jnp.einsum("msgc,isgc->gmi", left, right)
        rounded = lax.optimization_barrier(partial_sums.astype(jnp.bfloat16))
        return back, jnp.sum(rounded.astype(jnp.float32), axis=0)

    back_two, grad_two = lax.map(backward_second, (factor_two, upstream, moved))
    returned = back_two.transpose(1, 0, 2, 3)

    def backward_first(triple):
        weight, grads, block = triple
        flat = grads.reshape(B2, SEQS * D)
        grad_block = jnp.dot(weight.T, flat, preferred_element_type=jnp.float32).reshape(B2, SEQS, D)
        left = grads.astype(jnp.float32).reshape(B2, SEQS, N_CH, group_width)
        right = block.astype(jnp.float32).reshape(B2, SEQS, N_CH, group_width)
        partial_sums = jnp.einsum("ksgc,jsgc->gkj", left, right)
        rounded = lax.optimization_barrier(partial_sums.astype(jnp.bfloat16))
        return grad_block, jnp.sum(rounded.astype(jnp.float32), axis=0)

    grad_input, grad_one = lax.map(backward_first, (factor_one, returned, inputs))
    grad_input = grad_input.transpose(2, 0, 1, 3).reshape(SEQS, B1 * B2, D)
    d_values = (grad_input * gate.astype(jnp.float32)).astype(jnp.bfloat16)
    d_gate = (grad_input * values.astype(jnp.float32)).astype(jnp.bfloat16)
    return (d_values, d_gate, grad_one, grad_two)
```

```python
import jax
import jax.numpy as jnp
from jax import lax
from jax.experimental import pallas as pl
from jax.experimental.pallas import tpu as pltpu
from jax.sharding import PartitionSpec as P

MESH = pl.DeviceIdType.MESH
F32, BF16 = jnp.float32, jnp.bfloat16
N_CTX, N_CH = 32, 8
PAIRS = N_CTX // 2


def dot(a, b, dims):
    return lax.dot_general(a, b, (dims, ((), ())), preferred_element_type=F32)


class Place:
    def __init__(self):
        self.a = lax.axis_index("ctx")
        self.h = lax.axis_index("ch")
        self.y, self.xl = self.h // 2, self.h % 2
        self.xp = (self.a, self.piece(0, 1))
        self.yp = (self.a, self.piece(1, 0))
        self.ym = (self.a, self.piece(3, 0))

    def piece(self, dy, dx):
        xl = 1 - self.xl if dx else self.xl
        return lax.rem(self.y + dy, 4) * 2 + xl


def remote(src, dst, ssem, rsem, dev):
    return pltpu.make_async_remote_copy(
        src_ref=src, dst_ref=dst, send_sem=ssem, recv_sem=rsem, device_id=dev, device_id_type=MESH
    )


class Gather:
    def __init__(self, at, buf, ssem, rsem):
        self.at, self.buf, self.ssem, self.rsem = at, buf, ssem, rsem
        p = at.piece
        self.plan = (
            (p(0, 0), at.xp, p(0, 1)),
            (p(0, 0), at.yp, p(3, 0)),
            (p(0, 0), at.ym, p(1, 0)),
            (p(0, 1), at.yp, p(3, 1)),
            (p(0, 1), at.ym, p(1, 1)),
            (p(3, 0), at.yp, p(2, 0)),
            (p(1, 1), at.ym, p(2, 1)),
        )

    def copy(self, k, arrives=False):
        sent, dev, came = self.plan[k]
        ref = self.buf.at[came if arrives else sent]
        return remote(ref, ref, self.ssem.at[k], self.rsem.at[k], dev)

    def send(self, *ks):
        for k in ks:
            self.copy(k).start()

    def wait(self, *ks):
        for k in ks:
            self.copy(k, True).wait_recv()

    def drain(self):
        for k in range(7):
            self.copy(k).wait_send()


class Scatter:
    def __init__(self, at, part, got, ssem, rsem):
        self.at, self.part, self.got, self.ssem, self.rsem = at, part, got, ssem, rsem
        p = at.piece
        self.plan = (
            (p(2, 0), at.yp),
            (p(2, 1), at.ym),
            (p(1, 0), at.yp),
            (p(1, 1), at.yp),
            (p(3, 1), at.ym),
            (p(3, 0), at.ym),
            (p(0, 1), at.xp),
        )

    def copy(self, k):
        sent, dev = self.plan[k]
        return remote(self.part.at[sent], self.got.at[k], self.ssem.at[k], self.rsem.at[k], dev)

    def send(self, *ks):
        for k in ks:
            self.copy(k).start()

    def wait(self, *ks):
        for k in ks:
            self.copy(k).wait_recv()

    def add(self, piece, *ks):
        n = self.part.shape[1]

        def body(i, _):
            total = self.part[piece, i].astype(F32)
            for k in ks:
                total += self.got[k, i].astype(F32)
            self.part[piece, i] = total.astype(BF16)
            return 0

        lax.fori_loop(0, n, body, 0)

    def first(self):
        self.send(0, 1, 3, 5)

    def second(self):
        self.wait(0)
        self.add(self.at.piece(1, 0), 0)
        self.send(2)
        self.wait(1)
        self.add(self.at.piece(3, 1), 1)
        self.send(4)

    def third(self):
        self.wait(3, 4)
        self.add(self.at.piece(0, 1), 3, 4)
        self.send(6)

    def last(self, out):
        self.wait(2, 5, 6)
        mine = self.at.piece(0, 0)

        def body(i, _):
            total = self.part[mine, i].astype(F32)
            for k in (2, 5, 6):
                total += self.got[k, i].astype(F32)
            out[i] = total
            return 0

        lax.fori_loop(0, self.part.shape[1], body, 0)

    def drain(self):
        for k in range(7):
            self.copy(k).wait_send()


def kernel(
    v_hbm, g_hbm, c_hbm, f1_hbm, f2_hbm,
    dv_hbm, dg_hbm, o1_hbm, o2_hbm,
    val, gate, up, f1, f2, gated, back, sendb, ret, mix, mov, movt, part1, got1, part2, got2, out1, out2,
    lsem, osem, g2s, g2r, g1s, g1r, s1s, s1r, s2s, s2r, bs, br, ms, mr,
):
    at = Place()
    a, h = at.a, at.h
    pair0 = a // 2
    core = a % 2

    loads = []

    def load(src, dst):
        cp = pltpu.make_async_copy(src, dst, lsem.at[len(loads)])
        cp.start()
        loads.append(cp)
        return cp

    f2_in = load(f2_hbm, f2.at[h])
    f1_in = load(f1_hbm, f1.at[h])
    rest = []
    for s in range(2):
        lanes = pl.ds(128 * s, 128)
        rest.append(load(c_hbm.at[s], up.at[:, lanes]))
        rest.append(load(v_hbm.at[s], val.at[:, lanes]))
        rest.append(load(g_hbm.at[s], gate.at[:, lanes]))

    barrier = pltpu.get_barrier_semaphore()

    def greet(k, _):
        pl.semaphore_signal(barrier, inc=1, device_id=(lax.rem(a + k, N_CTX), h), device_id_type=MESH)
        return 0

    for dev in (at.xp, at.yp, at.ym):
        pl.semaphore_signal(barrier, inc=1, device_id=dev, device_id_type=MESH)
    lax.fori_loop(1, N_CTX, greet, 0)
    pl.semaphore_wait(barrier, N_CTX - 1 + 3)

    two = Gather(at, f2, g2s, g2r)
    one = Gather(at, f1, g1s, g1r)
    f2_in.wait()
    two.send(0, 1, 2)

    for cp in rest:
        cp.wait()

    def multiply(k, _):
        rows = pl.ds(pl.multiple_of(k * 512, 512), 512)
        gated[k] = (val[rows, :].astype(F32) * gate[rows, :].astype(F32)).astype(BF16)
        return 0

    lax.fori_loop(0, 8, multiply, 0)

    two.wait(0)
    two.send(3, 4)
    two.wait(1)
    two.send(5)
    two.wait(4)
    two.send(6)
    f1_in.wait()
    one.send(0, 1, 2)
    two.wait(2, 3, 5, 6)

    def back_block(k, _):
        w = f2[:, k].reshape(256, 256)
        u = up[pl.ds(pl.multiple_of(k * 256, 256), 256), :]
        back[k] = dot(w, u, ((0,), (0,))).astype(BF16)
        return 0

    lax.fori_loop(0, 16, back_block, 0)

    r = lax.broadcasted_iota(jnp.int32, (256, 256), 0)
    c = lax.broadcasted_iota(jnp.int32, (256, 256), 1)
    swap = jnp.where(((r >> 4) == (c & 15)) & ((r & 15) == (c >> 4)), 1.0, 0.0).astype(BF16)

    def back_copy(dst, slot):
        return remote(
            sendb.at[dst], ret.at[:, pl.ds(pl.multiple_of(16 * slot, 16), 16), :], bs.at[dst], br.at[slot], (dst, h)
        )

    def back_send(k, _):
        p = lax.rem(pair0 + k, PAIRS)
        x = back[:, pl.ds(pl.multiple_of(16 * p, 16), 16), :].reshape(256, 256)
        t = dot(swap, x, ((1,), (0,))).astype(BF16).reshape(2, 8, 16, 256)
        sendb[2 * p] = t[0]
        sendb[2 * p + 1] = t[1]

        @pl.when(k > 0)
        def _():
            back_copy(2 * p + core, a).start()

        back_copy(2 * p + 1 - core, a).start()
        return 0

    lax.fori_loop(0, PAIRS, back_send, 0)
    ret[:, pl.ds(pl.multiple_of(16 * a, 16), 16), :] = sendb[a]

    one.wait(0)
    one.send(3, 4)
    one.wait(1)
    one.send(5)
    one.wait(4)
    one.send(6)
    one.wait(2, 3, 5, 6)

    def mix_block(i, _):
        mix[i] = dot(f1[:, i].reshape(512, 512), gated[i], ((1,), (0,))).astype(BF16)
        return 0

    lax.fori_loop(0, 8, mix_block, 0)

    def mix_copy(dst, slot):
        return remote(
            mix.at[:, pl.ds(pl.multiple_of(16 * dst, 16), 16), :], mov.at[slot], ms.at[dst], mr.at[slot], (dst, h)
        )

    def mix_send(k, _):
        p = lax.rem(pair0 + k, PAIRS)

        @pl.when(k > 0)
        def _():
            mix_copy(2 * p + core, a).start()

        mix_copy(2 * p + 1 - core, a).start()
        return 0

    lax.fori_loop(0, PAIRS, mix_send, 0)
    mov[a] = mix[:, pl.ds(pl.multiple_of(16 * a, 16), 16), :]

    def back_wait(k, _):
        src = lax.rem(a + k, N_CTX)
        back_copy(src, src).wait_recv()
        return 0

    lax.fori_loop(1, N_CTX, back_wait, 0)

    def first_block(i, _):
        part1[:, i] = dot(ret[i], gated[i], ((1,), (1,))).astype(BF16).reshape(8, 64, 512)
        grad = dot(f1[:, i].reshape(512, 512), ret[i], ((0,), (0,)))
        rows = pl.ds(pl.multiple_of(i * 512, 512), 512)
        v, g = val[rows, :].astype(F32), gate[rows, :].astype(F32)
        val[rows, :] = (grad * g).astype(BF16)
        gate[rows, :] = (grad * v).astype(BF16)
        return 0

    lax.fori_loop(0, 8, first_block, 0)

    rs1 = Scatter(at, part1, got1, s1s, s1r)
    rs2 = Scatter(at, part2, got2, s2s, s2r)
    rs1.first()
    stores = []

    def store(src, dst):
        cp = pltpu.make_async_copy(src, dst, osem.at[len(stores)])
        cp.start()
        stores.append(cp)

    for s in range(2):
        lanes = pl.ds(128 * s, 128)
        store(val.at[:, lanes], dv_hbm.at[s])
        store(gate.at[:, lanes], dg_hbm.at[s])

    def mix_take(k, _):
        p = lax.rem(pair0 + PAIRS - k, PAIRS)

        @pl.when(k > 0)
        def _():
            mix_copy(2 * p + core, 2 * p + core).wait_recv()

        mix_copy(2 * p + 1 - core, 2 * p + 1 - core).wait_recv()
        x = mov[pl.ds(2 * p, 2)].reshape(256, 256)
        t = dot(swap, x, ((1,), (0,))).astype(BF16).reshape(16, 16, 256)
        movt[:, pl.ds(pl.multiple_of(16 * p, 16), 16), :] = t
        return 0

    lax.fori_loop(0, 4, mix_take, 0)
    rs1.second()
    lax.fori_loop(4, 8, mix_take, 0)
    rs1.third()
    lax.fori_loop(8, PAIRS, mix_take, 0)

    def second_block(k, _):
        u = up[pl.ds(pl.multiple_of(k * 256, 256), 256), :]
        part2[:, k] = dot(u, movt[k], ((1,), (1,))).astype(BF16).reshape(8, 32, 256)
        return 0

    lax.fori_loop(0, 16, second_block, 0)
    rs2.first()
    rs1.last(out1)
    store(out1, o1_hbm)
    rs2.second()
    rs2.third()
    rs2.last(out2)
    store(out2, o2_hbm)

    def drain(k, _):
        dst = lax.rem(a + k, N_CTX)
        back_copy(dst, a).wait_send()
        mix_copy(dst, a).wait_send()
        return 0

    lax.fori_loop(1, N_CTX, drain, 0)
    for x in (one, two, rs1, rs2):
        x.drain()
    for cp in stores:
        cp.wait()


def per_device(values, gate, cotangent, factor_one, factor_two):
    vm = pltpu.VMEM
    dma = pltpu.SemaphoreType.DMA
    shapes = (
        jax.ShapeDtypeStruct(values.shape, BF16),
        jax.ShapeDtypeStruct(values.shape, BF16),
        jax.ShapeDtypeStruct(factor_one.shape, F32),
        jax.ShapeDtypeStruct(factor_two.shape, F32),
    )
    scratch = [
        vm((4096, 256), BF16), vm((4096, 256), BF16), vm((4096, 256), BF16),
        vm((8, 8, 64, 512), BF16), vm((8, 16, 32, 256), BF16),
        vm((8, 512, 256), BF16),
        vm((16, 256, 256), BF16),
        vm((32, 8, 16, 256), BF16),
        vm((8, 512, 256), BF16),
        vm((8, 512, 256), BF16),
        vm((32, 8, 16, 256), BF16),
        vm((16, 256, 256), BF16),
        vm((8, 8, 64, 512), BF16), vm((7, 8, 64, 512), BF16),
        vm((8, 16, 32, 256), BF16), vm((7, 16, 32, 256), BF16),
        vm((8, 64, 512), F32), vm((16, 32, 256), F32),
        dma((8,)), dma((6,)),
        dma((7,)), dma((7,)), dma((7,)), dma((7,)), dma((7,)), dma((7,)), dma((7,)), dma((7,)),
        dma((32,)), dma((32,)), dma((32,)), dma((32,)),
    ]
    anywhere = pl.BlockSpec(memory_space=pl.ANY)
    return pl.pallas_call(
        kernel,
        out_shape=shapes,
        in_specs=[anywhere] * 5,
        out_specs=(anywhere,) * 4,
        scratch_shapes=scratch,
        compiler_params=pltpu.CompilerParams(
            collective_id=0, has_side_effects=True, vmem_limit_bytes=56 * 1024 * 1024
        ),
        name="monarch_backward",
    )(values, gate, cotangent, factor_one, factor_two)


def solution(mesh):
    tokens = P(None, "ctx", "ch")
    rows = P("ctx", "ch", None)
    return jax.shard_map(
        per_device,
        mesh=mesh,
        in_specs=(tokens, tokens, tokens, rows, rows),
        out_specs=(tokens, tokens, rows, rows),
        check_vma=False,
    )
```

```python
import jax
import jax.numpy as jnp
from jax import lax
from jax.experimental import pallas as pl
from jax.experimental.pallas import tpu as pltpu
from jax.sharding import PartitionSpec as P

MESH = pl.DeviceIdType.MESH
F32, BF16 = jnp.float32, jnp.bfloat16
N_CTX, N_CH = 32, 8
PAIRS = N_CTX // 2


def dot(a, b, dims):
    return lax.dot_general(a, b, (dims, ((), ())), preferred_element_type=F32)


class Place:
    def __init__(self):
        self.a = lax.axis_index("ctx")
        self.h = lax.axis_index("ch")
        self.y, self.xl = self.h // 2, self.h % 2
        self.xp = (self.a, self.piece(0, 1))
        self.yp = (self.a, self.piece(1, 0))
        self.ym = (self.a, self.piece(3, 0))

    def piece(self, dy, dx):
        xl = 1 - self.xl if dx else self.xl
        return lax.rem(self.y + dy, 4) * 2 + xl


def remote(src, dst, ssem, rsem, dev):
    return pltpu.make_async_remote_copy(
        src_ref=src, dst_ref=dst, send_sem=ssem, recv_sem=rsem, device_id=dev, device_id_type=MESH
    )


class Gather:
    def __init__(self, at, buf, ssem, rsem):
        self.at, self.buf, self.ssem, self.rsem = at, buf, ssem, rsem
        p = at.piece
        self.plan = (
            (p(0, 0), at.xp, p(0, 1)),
            (p(0, 0), at.yp, p(3, 0)),
            (p(0, 0), at.ym, p(1, 0)),
            (p(0, 1), at.yp, p(3, 1)),
            (p(0, 1), at.ym, p(1, 1)),
            (p(3, 0), at.yp, p(2, 0)),
            (p(1, 1), at.ym, p(2, 1)),
        )

    def copy(self, k, arrives=False):
        sent, dev, came = self.plan[k]
        ref = self.buf.at[came if arrives else sent]
        return remote(ref, ref, self.ssem.at[k], self.rsem.at[k], dev)

    def send(self, *ks):
        for k in ks:
            self.copy(k).start()

    def wait(self, *ks):
        for k in ks:
            self.copy(k, True).wait_recv()

    def drain(self):
        for k in range(7):
            self.copy(k).wait_send()


class Scatter:
    def __init__(self, at, part, got, ssem, rsem):
        self.at, self.part, self.got, self.ssem, self.rsem = at, part, got, ssem, rsem
        p = at.piece
        self.plan = (
            (p(2, 0), at.yp),
            (p(2, 1), at.ym),
            (p(1, 0), at.yp),
            (p(1, 1), at.yp),
            (p(3, 1), at.ym),
            (p(3, 0), at.ym),
            (p(0, 1), at.xp),
        )

    def copy(self, k):
        sent, dev = self.plan[k]
        return remote(self.part.at[sent], self.got.at[k], self.ssem.at[k], self.rsem.at[k], dev)

    def send(self, *ks):
        for k in ks:
            self.copy(k).start()

    def wait(self, *ks):
        for k in ks:
            self.copy(k).wait_recv()

    def add(self, piece, *ks):
        n = self.part.shape[1]

        def body(i, _):
            total = self.part[piece, i].astype(F32)
            for k in ks:
                total += self.got[k, i].astype(F32)
            self.part[piece, i] = total.astype(BF16)
            return 0

        lax.fori_loop(0, n, body, 0)

    def first(self):
        self.send(0, 1, 3, 5)

    def second(self):
        self.wait(0)
        self.add(self.at.piece(1, 0), 0)
        self.send(2)
        self.wait(1)
        self.add(self.at.piece(3, 1), 1)
        self.send(4)

    def third(self):
        self.wait(3, 4)
        self.add(self.at.piece(0, 1), 3, 4)
        self.send(6)

    def last(self, out):
        self.wait(2, 5, 6)
        mine = self.at.piece(0, 0)

        def body(i, _):
            total = self.part[mine, i].astype(F32)
            for k in (2, 5, 6):
                total += self.got[k, i].astype(F32)
            out[i] = total
            return 0

        lax.fori_loop(0, self.part.shape[1], body, 0)

    def drain(self):
        for k in range(7):
            self.copy(k).wait_send()


def kernel(
    v_hbm, g_hbm, c_hbm, f1_hbm, f2_hbm,
    dv_hbm, dg_hbm, o1_hbm, o2_hbm,
    val, gate, up, f1, f2_own, f2_far, f2_near, gated, back, sendb, ret, mix, mov, movt,
    part1, got1, part2f, got2f, part2n, got2n, out1, out2f, out2n, out2,
    lsem, osem, g2fs, g2fr, g2ns, g2nr, g1s, g1r, s1s, s1r, s2fs, s2fr, s2ns, s2nr, bs, br, ms, mr,
):
    at = Place()
    a, h = at.a, at.h
    z, xh, core = a // 4, (a // 2) % 2, a % 2
    pair0 = a // 2

    loads = []

    def load(src, dst):
        cp = pltpu.make_async_copy(src, dst, lsem.at[len(loads)])
        cp.start()
        loads.append(cp)
        return cp

    f2_in = load(f2_hbm, f2_own)
    f1_in = load(f1_hbm, f1.at[h])
    rest = []
    for s in range(2):
        lanes = pl.ds(128 * s, 128)
        rest.append(load(c_hbm.at[s], up.at[:, lanes]))
        rest.append(load(v_hbm.at[s], val.at[:, lanes]))
        rest.append(load(g_hbm.at[s], gate.at[:, lanes]))

    barrier = pltpu.get_barrier_semaphore()

    def greet(k, _):
        pl.semaphore_signal(barrier, inc=1, device_id=(lax.rem(a + k, N_CTX), h), device_id_type=MESH)
        return 0

    for dev in (at.xp, at.yp, at.ym):
        pl.semaphore_signal(barrier, inc=1, device_id=dev, device_id_type=MESH)
    lax.fori_loop(1, N_CTX, greet, 0)
    pl.semaphore_wait(barrier, N_CTX - 1 + 3)

    far = Gather(at, f2_far, g2fs, g2fr)
    near = Gather(at, f2_near, g2ns, g2nr)
    one = Gather(at, f1, g1s, g1r)

    f2_in.wait()
    turn = lax.rem(256 - 32 * lax.rem(z + 3, 8), 256)

    def turn_block(k, _):
        x = pltpu.roll(f2_own[k].astype(F32), turn, 1).astype(BF16)
        f2_far[h, k] = x[:, :128]
        f2_near[h, k] = x[:, 128:]
        return 0

    lax.fori_loop(0, 16, turn_block, 0)
    far.send(0, 1, 2)

    for cp in rest:
        cp.wait()

    def multiply(k, _):
        rows = pl.ds(pl.multiple_of(k * 512, 512), 512)
        gated[k] = (val[rows, :].astype(F32) * gate[rows, :].astype(F32)).astype(BF16)
        return 0

    lax.fori_loop(0, 8, multiply, 0)

    far.wait(0)
    far.send(3, 4)
    far.wait(1)
    far.send(5)
    far.wait(4)
    far.send(6)
    near.send(0, 1, 2)
    far.wait(2, 3, 5, 6)

    r = lax.broadcasted_iota(jnp.int32, (256, 256), 0)
    c = lax.broadcasted_iota(jnp.int32, (256, 256), 1)
    swap = jnp.where(((r >> 4) == (c & 15)) & ((r & 15) == (c >> 4)), 1.0, 0.0).astype(BF16)

    def back_copy(dst, slot):
        return remote(
            sendb.at[dst], ret.at[:, pl.ds(pl.multiple_of(16 * slot, 16), 16), :], bs.at[dst], br.at[slot], (dst, h)
        )

    def back_half(w_ref, first):
        def block(k, _):
            w = w_ref[:, k].reshape(256, 128)
            u = up[pl.ds(pl.multiple_of(k * 256, 256), 256), :]
            back[k] = dot(w, u, ((0,), (0,))).astype(BF16)
            return 0

        lax.fori_loop(0, 16, block, 0)

        def send(k, _):
            xt = lax.rem(xh + k, 2)
            p = lax.rem(z + first + k // 2, 8) * 2 + xt
            row = pl.multiple_of((k // 2) * 32 + xt * 16, 16)
            x = back[:, pl.ds(row, 16), :].reshape(256, 256)
            t = dot(swap, x, ((1,), (0,))).astype(BF16).reshape(2, 8, 16, 256)
            sendb[2 * p] = t[0]
            sendb[2 * p + 1] = t[1]

            @pl.when(p != pair0)
            def _():
                back_copy(2 * p + core, a).start()

            back_copy(2 * p + 1 - core, a).start()
            return 0

        lax.fori_loop(0, 8, send, 0)

    back_half(f2_far, 3)
    near.wait(0)
    near.send(3, 4)
    near.wait(1)
    near.send(5)
    near.wait(4)
    near.send(6)
    f1_in.wait()
    one.send(0, 1, 2)
    near.wait(2, 3, 5, 6)
    back_half(f2_near, 7)
    ret[:, pl.ds(pl.multiple_of(16 * a, 16), 16), :] = sendb[a]

    one.wait(0)
    one.send(3, 4)
    one.wait(1)
    one.send(5)
    one.wait(4)
    one.send(6)
    one.wait(2, 3, 5, 6)

    def mix_block(i, _):
        mix[i] = dot(f1[:, i].reshape(512, 512), gated[i], ((1,), (0,))).astype(BF16)
        return 0

    lax.fori_loop(0, 8, mix_block, 0)

    def mix_copy(dst, slot):
        return remote(
            mix.at[:, pl.ds(pl.multiple_of(16 * dst, 16), 16), :], mov.at[slot], ms.at[dst], mr.at[slot], (dst, h)
        )

    def mix_send(k, _):
        p = lax.rem(z + 3 + k // 2, 8) * 2 + lax.rem(xh + k, 2)

        @pl.when(p != pair0)
        def _():
            mix_copy(2 * p + core, a).start()

        mix_copy(2 * p + 1 - core, a).start()
        return 0

    lax.fori_loop(0, PAIRS, mix_send, 0)
    mov[a] = mix[:, pl.ds(pl.multiple_of(16 * a, 16), 16), :]

    def back_wait(k, _):
        src = lax.rem(a + k, N_CTX)
        back_copy(src, src).wait_recv()
        return 0

    lax.fori_loop(1, N_CTX, back_wait, 0)

    def grad_one_block(i, _):
        part1[:, i] = dot(ret[i], gated[i], ((1,), (1,))).astype(BF16).reshape(8, 64, 512)
        return 0

    lax.fori_loop(0, 8, grad_one_block, 0)
    rs1 = Scatter(at, part1, got1, s1s, s1r)
    rs2f = Scatter(at, part2f, got2f, s2fs, s2fr)
    rs2n = Scatter(at, part2n, got2n, s2ns, s2nr)
    rs1.first()

    def grad_input_block(i, _):
        grad = dot(f1[:, i].reshape(512, 512), ret[i], ((0,), (0,)))
        rows = pl.ds(pl.multiple_of(i * 512, 512), 512)
        v, g = val[rows, :].astype(F32), gate[rows, :].astype(F32)
        val[rows, :] = (grad * g).astype(BF16)
        gate[rows, :] = (grad * v).astype(BF16)
        return 0

    lax.fori_loop(0, 8, grad_input_block, 0)
    stores = []

    def store(src, dst):
        cp = pltpu.make_async_copy(src, dst, osem.at[len(stores)])
        cp.start()
        stores.append(cp)

    for s in range(2):
        lanes = pl.ds(128 * s, 128)
        store(val.at[:, lanes], dv_hbm.at[s])
        store(gate.at[:, lanes], dg_hbm.at[s])

    def second_half(part, last):
        def take(k, _):
            zo = last + 8 - k // 2
            xt = lax.rem(xh + k, 2)
            p = lax.rem(z + zo, 8) * 2 + xt

            @pl.when(p != pair0)
            def _():
                mix_copy(2 * p + core, 2 * p + core).wait_recv()

            mix_copy(2 * p + 1 - core, 2 * p + 1 - core).wait_recv()
            x = mov[pl.ds(2 * p, 2)].reshape(256, 256)
            t = dot(swap, x, ((1,), (0,))).astype(BF16).reshape(16, 16, 256)
            row = pl.multiple_of((3 - k // 2) * 32 + xt * 16, 16)
            movt[:, pl.ds(row, 16), :] = t
            return 0

        lax.fori_loop(0, 8, take, 0)

        def block(k, _):
            u = up[pl.ds(pl.multiple_of(k * 256, 256), 256), :]
            part[:, k] = dot(u, movt[k], ((1,), (1,))).astype(BF16).reshape(8, 32, 128)
            return 0

        lax.fori_loop(0, 16, block, 0)

    rs1.second()
    second_half(part2f, 5)
    rs2f.first()
    rs1.third()
    rs2f.second()
    second_half(part2n, 9)
    rs2n.first()
    rs1.last(out1)
    store(out1, o1_hbm)
    rs2f.third()
    rs2n.second()
    rs2f.last(out2f)
    rs2n.third()
    rs2n.last(out2n)
    unturn = 32 * lax.rem(z + 2, 8)

    def unturn_block(k, _):
        out2[k] = pltpu.roll(jnp.concatenate([out2f[k], out2n[k]], axis=1), unturn, 1)
        return 0

    lax.fori_loop(0, 16, unturn_block, 0)
    store(out2, o2_hbm)

    def drain(k, _):
        dst = lax.rem(a + k, N_CTX)
        back_copy(dst, a).wait_send()
        mix_copy(dst, a).wait_send()
        return 0

    lax.fori_loop(1, N_CTX, drain, 0)
    for x in (far, near, one, rs1, rs2f, rs2n):
        x.drain()
    for cp in stores:
        cp.wait()


def per_device(values, gate, cotangent, factor_one, factor_two):
    vm = pltpu.VMEM
    dma = pltpu.SemaphoreType.DMA
    shapes = (
        jax.ShapeDtypeStruct(values.shape, BF16),
        jax.ShapeDtypeStruct(values.shape, BF16),
        jax.ShapeDtypeStruct(factor_one.shape, F32),
        jax.ShapeDtypeStruct(factor_two.shape, F32),
    )
    scratch = [
        vm((4096, 256), BF16), vm((4096, 256), BF16), vm((4096, 256), BF16),
        vm((8, 8, 64, 512), BF16),
        vm((16, 32, 256), BF16), vm((8, 16, 32, 128), BF16), vm((8, 16, 32, 128), BF16),
        vm((8, 512, 256), BF16),
        vm((16, 128, 256), BF16),
        vm((32, 8, 16, 256), BF16),
        vm((8, 512, 256), BF16),
        vm((8, 512, 256), BF16),
        vm((32, 8, 16, 256), BF16),
        vm((16, 128, 256), BF16),
        vm((8, 8, 64, 512), BF16), vm((7, 8, 64, 512), BF16),
        vm((8, 16, 32, 128), BF16), vm((7, 16, 32, 128), BF16),
        vm((8, 16, 32, 128), BF16), vm((7, 16, 32, 128), BF16),
        vm((8, 64, 512), F32), vm((16, 32, 128), F32), vm((16, 32, 128), F32), vm((16, 32, 256), F32),
        dma((8,)), dma((6,)),
        *[dma((7,)) for _ in range(12)],
        dma((32,)), dma((32,)), dma((32,)), dma((32,)),
    ]
    anywhere = pl.BlockSpec(memory_space=pl.ANY)
    return pl.pallas_call(
        kernel,
        out_shape=shapes,
        in_specs=[anywhere] * 5,
        out_specs=(anywhere,) * 4,
        scratch_shapes=scratch,
        compiler_params=pltpu.CompilerParams(
            collective_id=0, has_side_effects=True, vmem_limit_bytes=56 * 1024 * 1024
        ),
        name="monarch_backward",
    )(values, gate, cotangent, factor_one, factor_two)


def solution(mesh):
    tokens = P(None, "ctx", "ch")
    rows = P("ctx", "ch", None)
    return jax.shard_map(
        per_device,
        mesh=mesh,
        in_specs=(tokens, tokens, tokens, rows, rows),
        out_specs=(tokens, tokens, rows, rows),
        check_vma=False,
    )
```

```python
import jax
import jax.numpy as jnp
from jax import lax
from jax.experimental import pallas as pl
from jax.experimental.pallas import tpu as pltpu
from jax.sharding import PartitionSpec as P

MESH = pl.DeviceIdType.MESH
F32, BF16 = jnp.float32, jnp.bfloat16
N_CTX, N_CH = 32, 8
PAIRS = N_CTX // 2


def dot(a, b, dims):
    return lax.dot_general(a, b, (dims, ((), ())), preferred_element_type=F32)


class Place:
    def __init__(self):
        self.a = lax.axis_index("ctx")
        self.h = lax.axis_index("ch")
        self.y, self.xl = self.h // 2, self.h % 2
        self.xp = (self.a, self.piece(0, 1))
        self.yp = (self.a, self.piece(1, 0))
        self.ym = (self.a, self.piece(3, 0))

    def piece(self, dy, dx):
        xl = 1 - self.xl if dx else self.xl
        return lax.rem(self.y + dy, 4) * 2 + xl


def remote(src, dst, ssem, rsem, dev):
    return pltpu.make_async_remote_copy(
        src_ref=src, dst_ref=dst, send_sem=ssem, recv_sem=rsem, device_id=dev, device_id_type=MESH
    )


class Gather:
    def __init__(self, at, buf, ssem, rsem, start=0, size=None):
        self.at, self.buf, self.ssem, self.rsem = at, buf, ssem, rsem
        self.blocks = pl.ds(start, buf.shape[1] if size is None else size)
        p = at.piece
        self.plan = (
            (p(0, 0), at.xp, p(0, 1)),
            (p(0, 0), at.yp, p(3, 0)),
            (p(0, 0), at.ym, p(1, 0)),
            (p(0, 1), at.yp, p(3, 1)),
            (p(0, 1), at.ym, p(1, 1)),
            (p(3, 0), at.yp, p(2, 0)),
            (p(1, 1), at.ym, p(2, 1)),
        )

    def copy(self, k, arrives=False):
        sent, dev, came = self.plan[k]
        ref = self.buf.at[came if arrives else sent, self.blocks]
        return remote(ref, ref, self.ssem.at[k], self.rsem.at[k], dev)

    def send(self, *ks):
        for k in ks:
            self.copy(k).start()

    def wait(self, *ks):
        for k in ks:
            self.copy(k, True).wait_recv()

    def relay(self):
        self.wait(0)
        self.send(3, 4)
        self.wait(1)
        self.send(5)
        self.wait(4)
        self.send(6)

    def drain(self):
        for k in range(7):
            self.copy(k).wait_send()


class Direct:
    ORDER = (1, 4, 5, 2, 6, 3, 7)

    def __init__(self, at, part, got, ssem, rsem):
        self.at, self.part, self.got, self.ssem, self.rsem = at, part, got, ssem, rsem

    def copy(self, d):
        there = self.at.piece(d // 2, d % 2)
        if self.got is None:
            mine = self.part.at[self.at.piece(0, 0)]
            return remote(mine, mine, self.ssem.at[d - 1], self.rsem.at[d - 1], (self.at.a, there))
        return remote(self.part.at[there], self.got.at[d - 1], self.ssem.at[d - 1], self.rsem.at[d - 1], (self.at.a, there))

    def send(self):
        for d in self.ORDER:
            self.copy(d).start()

    def wait(self):
        for d in self.ORDER:
            if self.got is None:
                came = self.part.at[self.at.piece((8 - d // 2) % 4, d % 2)]
                remote(came, came, self.ssem.at[d - 1], self.rsem.at[d - 1], self.at.xp).wait_recv()
            else:
                self.copy(d).wait_recv()

    def last(self, out):
        self.wait()
        mine = self.at.piece(0, 0)

        def body(i, _):
            total = self.part[mine, i].astype(F32)
            for k in range(7):
                total += self.got[k, i].astype(F32)
            out[i] = total
            return 0

        lax.fori_loop(0, self.part.shape[1], body, 0)

    def drain(self):
        for d in self.ORDER:
            self.copy(d).wait_send()


class Scatter:
    def __init__(self, at, part, got, ssem, rsem, start=0, size=None):
        self.at, self.part, self.got, self.ssem, self.rsem = at, part, got, ssem, rsem
        self.start, self.size = start, part.shape[1] if size is None else size
        self.blocks = pl.ds(self.start, self.size)
        p = at.piece
        self.plan = (
            (p(2, 0), at.yp),
            (p(2, 1), at.ym),
            (p(1, 0), at.yp),
            (p(1, 1), at.yp),
            (p(3, 1), at.ym),
            (p(3, 0), at.ym),
            (p(0, 1), at.xp),
        )

    def copy(self, k):
        sent, dev = self.plan[k]
        return remote(
            self.part.at[sent, self.blocks], self.got.at[k, self.blocks], self.ssem.at[k], self.rsem.at[k], dev
        )

    def send(self, *ks):
        for k in ks:
            self.copy(k).start()

    def wait(self, *ks):
        for k in ks:
            self.copy(k).wait_recv()

    def add(self, piece, *ks):
        def body(i, _):
            total = self.part[piece, i].astype(F32)
            for k in ks:
                total += self.got[k, i].astype(F32)
            self.part[piece, i] = total.astype(BF16)
            return 0

        lax.fori_loop(self.start, self.start + self.size, body, 0)

    def first(self):
        self.send(0, 1, 3, 5)

    def second(self):
        self.wait(1)
        self.add(self.plan[4][0], 1)
        self.send(4)
        self.wait(0)
        self.add(self.plan[2][0], 0)
        self.send(2)

    def third(self):
        self.wait(3, 4)
        self.add(self.plan[6][0], 3, 4)
        self.send(6)

    def last(self, out):
        self.wait(2, 5, 6)
        mine = self.at.piece(0, 0)

        def body(i, _):
            total = self.part[mine, i].astype(F32)
            for k in (2, 5, 6):
                total += self.got[k, i].astype(F32)
            out[i] = total
            return 0

        lax.fori_loop(self.start, self.start + self.size, body, 0)

    def drain(self):
        for k in range(7):
            self.copy(k).wait_send()


def kernel(
    v_hbm, g_hbm, c_hbm, f1_hbm, f2_hbm,
    dv_hbm, dg_hbm, o1_hbm, o2_hbm,
    val, gate, up, f1, f2_own, f2_a, f2_b, f2_near, gated, back, sendb, ret, mix, mov, movt,
    part1, got1, part2n, got2n, part2c, got2c, part2d, got2d, out1, out2n, out2c, out2d, out2,
    lsem, osem, g2as, g2ar, g2bs, g2br, g2ns, g2nr, g1as, g1ar, g1bs, g1br,
    s1as, s1ar, s1bs, s1br, s2ns, s2nr, s2cs, s2cr, s2ds, s2dr, bs, br, ms, mr,
):
    at = Place()
    a, h = at.a, at.h
    z, xh, core = a // 4, (a // 2) % 2, a % 2
    pair0 = a // 2

    loads = []

    def load(src, dst):
        cp = pltpu.make_async_copy(src, dst, lsem.at[len(loads)])
        cp.start()
        loads.append(cp)
        return cp

    f2_in = load(f2_hbm, f2_own)
    f1_in = load(f1_hbm, f1.at[h])
    rest = []
    for s in range(2):
        lanes = pl.ds(128 * s, 128)
        rest.append(load(c_hbm.at[s], up.at[:, lanes]))
        rest.append(load(v_hbm.at[s], val.at[:, lanes]))
        rest.append(load(g_hbm.at[s], gate.at[:, lanes]))

    barrier = pltpu.get_barrier_semaphore()

    def greet(k, _):
        pl.semaphore_signal(barrier, inc=1, device_id=(lax.rem(a + k, N_CTX), h), device_id_type=MESH)
        return 0

    for d in range(1, N_CH):
        pl.semaphore_signal(barrier, inc=1, device_id=(a, at.piece(d // 2, d % 2)), device_id_type=MESH)
    lax.fori_loop(1, N_CTX, greet, 0)
    far_a = Direct(at, f2_a, None, g2as, g2ar)
    far_b = Direct(at, f2_b, None, g2bs, g2br)
    near = Gather(at, f2_near, g2ns, g2nr)
    one_a = Gather(at, f1, g1as, g1ar, 0, 4)
    one_b = Gather(at, f1, g1bs, g1br, 4, 4)

    f2_in.wait()
    turn = lax.rem(256 - 32 * lax.rem(z + 3, 8), 256)

    def turn_block(k, _):
        x = pltpu.roll(f2_own[2 * k].astype(F32), turn, 1)
        y = pltpu.roll(f2_own[2 * k + 1].astype(F32), turn, 1)
        f2_a[h, k] = jnp.concatenate([x[:, :64], y[:, :64]], axis=1).astype(BF16)
        f2_b[h, k] = jnp.concatenate([x[:, 64:128], y[:, 64:128]], axis=1).astype(BF16)
        f2_near[h, 2 * k] = x[:, 128:].astype(BF16)
        f2_near[h, 2 * k + 1] = y[:, 128:].astype(BF16)
        return 0

    lax.fori_loop(0, 8, turn_block, 0)
    pl.semaphore_wait(barrier, N_CTX - 1 + N_CH - 1)
    far_a.send()
    far_b.send()
    for cp in rest:
        cp.wait()

    def multiply(k, _):
        rows = pl.ds(pl.multiple_of(k * 512, 512), 512)
        gated[k] = (val[rows, :].astype(F32) * gate[rows, :].astype(F32)).astype(BF16)
        return 0

    lax.fori_loop(0, 8, multiply, 0)

    r = lax.broadcasted_iota(jnp.int32, (256, 256), 0)
    c = lax.broadcasted_iota(jnp.int32, (256, 256), 1)
    swap = jnp.where(((r >> 4) == (c & 15)) & ((r & 15) == (c >> 4)), 1.0, 0.0).astype(BF16)

    def back_copy(dst, src):
        row = lax.rem(src // 4 - dst // 4 + 14, 8) * 64 + lax.rem(src, 4) * 16
        return remote(sendb.at[dst], ret.at[:, pl.ds(pl.multiple_of(row, 16), 16), :], bs.at[dst], br.at[src], (dst, h))

    def upstream(k):
        return up[pl.ds(pl.multiple_of(k * 256, 256), 256), :]

    def back_send(first, row0, count):
        def send(k, _):
            xt = lax.rem(xh + k, 2)
            p = lax.rem(z + first + k // 2, 8) * 2 + xt
            row = pl.multiple_of(row0 + (k // 2) * 32 + xt * 16, 16)
            x = back[:, pl.ds(row, 16), :].reshape(256, 256)
            t = dot(swap, x, ((1,), (0,))).astype(BF16).reshape(2, 8, 16, 256)
            sendb[2 * p] = t[0]
            sendb[2 * p + 1] = t[1]

            @pl.when(p != pair0)
            def _():
                back_copy(2 * p + core, a).start()

            back_copy(2 * p + 1 - core, a).start()
            return 0

        lax.fori_loop(0, count, send, 0, unroll=2)

    def back_quarter(w_ref, first, row0):
        def block(k, _):
            w = w_ref[:, k].reshape(256, 128)
            back[2 * k, row0:row0 + 64] = dot(w[:, :64], upstream(2 * k), ((0,), (0,))).astype(BF16)
            back[2 * k + 1, row0:row0 + 64] = dot(w[:, 64:], upstream(2 * k + 1), ((0,), (0,))).astype(BF16)
            return 0

        lax.fori_loop(0, 8, block, 0, unroll=2)
        back_send(first, row0, 4)

    def back_near(k, _):
        back[k, 128:] = dot(f2_near[:, k].reshape(256, 128), upstream(k), ((0,), (0,))).astype(BF16)
        return 0

    far_a.wait()
    near.send(0, 1, 2)
    f1_in.wait()
    one_a.send(0, 1, 2)
    back_quarter(f2_a, 3, 0)
    far_b.wait()
    back_quarter(f2_b, 5, 64)
    near.wait(0)
    near.send(3, 4)
    one_a.wait(0)
    one_a.send(3, 4)
    near.wait(1)
    near.send(5)
    one_b.send(0, 1, 2)
    near.wait(4)
    near.send(6)
    one_a.wait(1)
    one_a.send(5)
    one_b.wait(0)
    one_b.send(3, 4)
    one_a.wait(4)
    one_a.send(6)
    one_b.wait(1)
    one_b.send(5)
    near.wait(2, 3, 5, 6)
    lax.fori_loop(0, 16, back_near, 0, unroll=4)
    back_send(7, 128, 8)
    ret[:, pl.ds(pl.multiple_of(384 + lax.rem(a, 4) * 16, 16), 16), :] = sendb[a]
    one_b.wait(4)
    one_b.send(6)

    def mix_block(i, _):
        mix[i] = dot(f1[:, i].reshape(512, 512), gated[i], ((1,), (0,))).astype(BF16)
        return 0

    def mix_copy(c, dst, slot):
        rows = pl.ds(pl.multiple_of(16 * dst, 16), 16)
        blocks = pl.ds(4 * c, 4)
        return remote(mix.at[blocks, rows, :], mov.at[slot, blocks], ms.at[c, dst], mr.at[c, slot], (dst, h))

    def mix_send(c, first, count):
        def send(k, _):
            p = lax.rem(z + first + k // 2, 8) * 2 + lax.rem(xh + k, 2)

            @pl.when(p != pair0)
            def _():
                mix_copy(c, 2 * p + core, a).start()

            mix_copy(c, 2 * p + 1 - core, a).start()
            return 0

        lax.fori_loop(0, count, send, 0)

    one_a.wait(2, 3, 5, 6)
    lax.fori_loop(0, 4, mix_block, 0, unroll=2)
    mix_send(0, 6, 12)

    def back_wait(k, _):
        src = lax.rem(a + k, N_CTX)
        back_copy(a, src).wait_recv()
        return 0

    lax.fori_loop(1, N_CTX, back_wait, 0)

    def grad_one_block(i, _):
        t = dot(ret[i], gated[i], ((1,), (1,))).astype(BF16).reshape(8, 64, 512)
        for q in range(8):
            part1[lax.rem(z + 2 + q, 8), i] = t[q]
        return 0

    def grad_input_block(i, _):
        w = jnp.concatenate([f1[lax.rem(z + 2 + q, 8), i] for q in range(8)], axis=0)
        grad = dot(w, ret[i], ((0,), (0,)))
        rows = pl.ds(pl.multiple_of(i * 512, 512), 512)
        v, g = val[rows, :].astype(F32), gate[rows, :].astype(F32)
        val[rows, :] = (grad * g).astype(BF16)
        gate[rows, :] = (grad * v).astype(BF16)
        return 0

    rs1a = Scatter(at, part1, got1, s1as, s1ar, 0, 4)
    rs1b = Scatter(at, part1, got1, s1bs, s1br, 4, 4)
    lax.fori_loop(0, 4, grad_one_block, 0, unroll=2)
    rs1a.first()
    one_b.wait(2, 3, 5, 6)
    lax.fori_loop(4, 8, mix_block, 0, unroll=2)
    mix_send(1, 6, 12)
    mov[a] = mix[:, pl.ds(pl.multiple_of(16 * a, 16), 16), :]
    lax.fori_loop(4, 8, grad_one_block, 0, unroll=2)
    rs1b.first()
    lax.fori_loop(0, 8, grad_input_block, 0, unroll=2)
    mix_send(0, 4, 4)
    mix_send(1, 4, 4)
    rs1a.second()
    stores = []

    def store(src, dst):
        cp = pltpu.make_async_copy(src, dst, osem.at[len(stores)])
        cp.start()
        stores.append(cp)

    for s in range(2):
        lanes = pl.ds(128 * s, 128)
        store(val.at[:, lanes], dv_hbm.at[s])
        store(gate.at[:, lanes], dg_hbm.at[s])

    def take(last, row0, count):
        def body(k, _):
            xt = lax.rem(xh + k, 2)
            p = lax.rem(z + last + 8 - k // 2, 8) * 2 + xt

            @pl.when(p != pair0)
            def _():
                mix_copy(0, 2 * p + core, 2 * p + core).wait_recv()
                mix_copy(1, 2 * p + core, 2 * p + core).wait_recv()

            mix_copy(0, 2 * p + 1 - core, 2 * p + 1 - core).wait_recv()
            mix_copy(1, 2 * p + 1 - core, 2 * p + 1 - core).wait_recv()
            x = mov[pl.ds(2 * p, 2)].reshape(256, 256)
            t = dot(swap, x, ((1,), (0,))).astype(BF16).reshape(16, 16, 256)
            row = pl.multiple_of(row0 - (k // 2) * 32 + xt * 16, 16)
            movt[:, pl.ds(row, 16), :] = t
            return 0

        lax.fori_loop(0, count, body, 0, unroll=2)

    def grad_two_near(k, _):
        t = dot(upstream(k), movt[k, 128:], ((1,), (1,))).astype(BF16)
        part2n[:, k] = t.reshape(8, 32, 128)
        return 0

    def grad_two_quarter(part, row0):
        def body(k, _):
            t = [dot(upstream(2 * k + e), movt[2 * k + e, row0:row0 + 64], ((1,), (1,))) for e in range(2)]
            part[:, k] = jnp.concatenate(t, axis=1).astype(BF16).reshape(8, 32, 128)
            return 0

        lax.fori_loop(0, 8, body, 0, unroll=2)

    rs2n = Scatter(at, part2n, got2n, s2ns, s2nr)
    rs2c = Scatter(at, part2c, got2c, s2cs, s2cr)
    rs2d = Direct(at, part2d, got2d, s2ds, s2dr)
    take(10, 224, 8)
    lax.fori_loop(0, 16, grad_two_near, 0, unroll=4)
    rs2n.first()
    rs1a.third()
    take(6, 96, 4)
    grad_two_quarter(part2c, 64)
    rs2c.first()
    rs1b.second()
    rs2n.second()
    rs2c.second()
    rs1b.third()
    take(4, 32, 4)
    grad_two_quarter(part2d, 0)
    rs2d.send()
    rs2n.third()
    rs2c.third()
    rs1a.last(out1)
    rs1b.last(out1)
    store(out1, o1_hbm)
    rs2n.last(out2n)
    rs2c.last(out2c)
    rs2d.last(out2d)
    unturn = 32 * lax.rem(z + 3, 8)

    def unturn_block(k, _):
        for e in range(2):
            lanes = slice(64 * e, 64 * e + 64)
            x = jnp.concatenate([out2d[k, :, lanes], out2c[k, :, lanes], out2n[2 * k + e]], axis=1)
            out2[2 * k + e] = pltpu.roll(x, unturn, 1)
        return 0

    lax.fori_loop(0, 8, unturn_block, 0)
    store(out2, o2_hbm)

    def drain(k, _):
        dst = lax.rem(a + k, N_CTX)
        back_copy(dst, a).wait_send()
        mix_copy(0, dst, a).wait_send()
        mix_copy(1, dst, a).wait_send()
        return 0

    lax.fori_loop(1, N_CTX, drain, 0)
    for x in (far_a, far_b, near, one_a, one_b, rs1a, rs1b, rs2n, rs2c, rs2d):
        x.drain()
    for cp in stores:
        cp.wait()


def per_device(values, gate, cotangent, factor_one, factor_two):
    vm = pltpu.VMEM
    dma = pltpu.SemaphoreType.DMA
    shapes = (
        jax.ShapeDtypeStruct(values.shape, BF16),
        jax.ShapeDtypeStruct(values.shape, BF16),
        jax.ShapeDtypeStruct(factor_one.shape, F32),
        jax.ShapeDtypeStruct(factor_two.shape, F32),
    )
    scratch = [
        vm((4096, 256), BF16), vm((4096, 256), BF16), vm((4096, 256), BF16),
        vm((8, 8, 64, 512), BF16),
        vm((16, 32, 256), BF16), vm((8, 8, 32, 128), BF16), vm((8, 8, 32, 128), BF16), vm((8, 16, 32, 128), BF16),
        vm((8, 512, 256), BF16),
        vm((16, 256, 256), BF16),
        vm((32, 8, 16, 256), BF16),
        vm((8, 512, 256), BF16),
        vm((8, 512, 256), BF16),
        vm((32, 8, 16, 256), BF16),
        vm((16, 256, 256), BF16),
        vm((8, 8, 64, 512), BF16), vm((7, 8, 64, 512), BF16),
        vm((8, 16, 32, 128), BF16), vm((7, 16, 32, 128), BF16),
        vm((8, 8, 32, 128), BF16), vm((7, 8, 32, 128), BF16),
        vm((8, 8, 32, 128), BF16), vm((7, 8, 32, 128), BF16),
        vm((8, 64, 512), F32),
        vm((16, 32, 128), F32), vm((8, 32, 128), F32), vm((8, 32, 128), F32), vm((16, 32, 256), F32),
        dma((8,)), dma((6,)),
        *[dma((7,)) for _ in range(20)],
        dma((32,)), dma((32,)), dma((2, 32)), dma((2, 32)),
    ]
    anywhere = pl.BlockSpec(memory_space=pl.ANY)
    return pl.pallas_call(
        kernel,
        out_shape=shapes,
        in_specs=[anywhere] * 5,
        out_specs=(anywhere,) * 4,
        scratch_shapes=scratch,
        compiler_params=pltpu.CompilerParams(
            collective_id=0, has_side_effects=True, vmem_limit_bytes=46 * 1024 * 1024
        ),
        name="monarch_backward",
    )(values, gate, cotangent, factor_one, factor_two)


def solution(mesh):
    tokens = P(None, "ctx", "ch")
    rows = P("ctx", "ch", None)
    return jax.shard_map(
        per_device,
        mesh=mesh,
        in_specs=(tokens, tokens, tokens, rows, rows),
        out_specs=(tokens, tokens, rows, rows),
        check_vma=False,
    )
```

```python
import jax
import jax.numpy as jnp
from jax import lax
from jax.experimental import pallas as pl
from jax.experimental.pallas import tpu as pltpu
from jax.sharding import PartitionSpec as P

MESH = pl.DeviceIdType.MESH
F32, BF16 = jnp.float32, jnp.bfloat16
N_CTX, N_CH = 32, 8
PAIRS = N_CTX // 2


def dot(a, b, dims):
    return lax.dot_general(a, b, (dims, ((), ())), preferred_element_type=F32)


class Place:
    def __init__(self):
        self.a = lax.axis_index("ctx")
        self.h = lax.axis_index("ch")
        self.y, self.xl = self.h // 2, self.h % 2
        self.xp = (self.a, self.piece(0, 1))
        self.yp = (self.a, self.piece(1, 0))
        self.ym = (self.a, self.piece(3, 0))

    def piece(self, dy, dx):
        xl = 1 - self.xl if dx else self.xl
        return lax.rem(self.y + dy, 4) * 2 + xl


def remote(src, dst, ssem, rsem, dev):
    return pltpu.make_async_remote_copy(
        src_ref=src, dst_ref=dst, send_sem=ssem, recv_sem=rsem, device_id=dev, device_id_type=MESH
    )


class Gather:
    def __init__(self, at, buf, ssem, rsem, start=0, size=None):
        self.at, self.buf, self.ssem, self.rsem = at, buf, ssem, rsem
        self.blocks = pl.ds(start, buf.shape[1] if size is None else size)
        p = at.piece
        self.plan = (
            (p(0, 0), at.xp, p(0, 1)),
            (p(0, 0), at.yp, p(3, 0)),
            (p(0, 0), at.ym, p(1, 0)),
            (p(0, 1), at.yp, p(3, 1)),
            (p(0, 1), at.ym, p(1, 1)),
            (p(3, 0), at.yp, p(2, 0)),
            (p(1, 1), at.ym, p(2, 1)),
        )

    def copy(self, k, arrives=False):
        sent, dev, came = self.plan[k]
        ref = self.buf.at[came if arrives else sent, self.blocks]
        return remote(ref, ref, self.ssem.at[k], self.rsem.at[k], dev)

    def send(self, *ks):
        for k in ks:
            self.copy(k).start()

    def wait(self, *ks):
        for k in ks:
            self.copy(k, True).wait_recv()

    def relay(self):
        self.wait(0)
        self.send(3, 4)
        self.wait(1)
        self.send(5)
        self.wait(4)
        self.send(6)

    def drain(self):
        for k in range(7):
            self.copy(k).wait_send()


class Direct:
    ORDER = (1, 4, 5, 2, 6, 3, 7)

    def __init__(self, at, part, got, ssem, rsem):
        self.at, self.part, self.got, self.ssem, self.rsem = at, part, got, ssem, rsem

    def copy(self, d):
        there = self.at.piece(d // 2, d % 2)
        if self.got is None:
            mine = self.part.at[self.at.piece(0, 0)]
            return remote(mine, mine, self.ssem.at[d - 1], self.rsem.at[d - 1], (self.at.a, there))
        return remote(self.part.at[there], self.got.at[d - 1], self.ssem.at[d - 1], self.rsem.at[d - 1], (self.at.a, there))

    def send(self):
        for d in self.ORDER:
            self.copy(d).start()

    def wait(self):
        for d in self.ORDER:
            if self.got is None:
                came = self.part.at[self.at.piece((8 - d // 2) % 4, d % 2)]
                remote(came, came, self.ssem.at[d - 1], self.rsem.at[d - 1], self.at.xp).wait_recv()
            else:
                self.copy(d).wait_recv()

    def last(self, out):
        self.wait()
        mine = self.at.piece(0, 0)

        def body(i, _):
            total = self.part[mine, i].astype(F32)
            for k in range(7):
                total += self.got[k, i].astype(F32)
            out[i] = total
            return 0

        lax.fori_loop(0, self.part.shape[1], body, 0)

    def drain(self):
        for d in self.ORDER:
            self.copy(d).wait_send()


class Scatter:
    def __init__(self, at, part, got, ssem, rsem, start=0, size=None):
        self.at, self.part, self.got, self.ssem, self.rsem = at, part, got, ssem, rsem
        self.start, self.size = start, part.shape[1] if size is None else size
        self.blocks = pl.ds(self.start, self.size)
        p = at.piece
        self.plan = (
            (p(2, 0), at.yp),
            (p(2, 1), at.ym),
            (p(1, 0), at.yp),
            (p(1, 1), at.yp),
            (p(3, 1), at.ym),
            (p(3, 0), at.ym),
            (p(0, 1), at.xp),
        )

    def copy(self, k):
        sent, dev = self.plan[k]
        return remote(
            self.part.at[sent, self.blocks], self.got.at[k, self.blocks], self.ssem.at[k], self.rsem.at[k], dev
        )

    def send(self, *ks):
        for k in ks:
            self.copy(k).start()

    def wait(self, *ks):
        for k in ks:
            self.copy(k).wait_recv()

    def add(self, piece, *ks):
        def body(i, _):
            total = self.part[piece, i].astype(F32)
            for k in ks:
                total += self.got[k, i].astype(F32)
            self.part[piece, i] = total.astype(BF16)
            return 0

        lax.fori_loop(self.start, self.start + self.size, body, 0)

    def first(self):
        self.send(0, 1, 3, 5)

    def second(self):
        self.wait(1)
        self.add(self.plan[4][0], 1)
        self.send(4)
        self.wait(0)
        self.add(self.plan[2][0], 0)
        self.send(2)

    def third(self):
        self.wait(3, 4)
        self.add(self.plan[6][0], 3, 4)
        self.send(6)

    def last(self, out):
        self.wait(2, 5, 6)
        mine = self.at.piece(0, 0)

        def body(i, _):
            total = self.part[mine, i].astype(F32)
            for k in (2, 5, 6):
                total += self.got[k, i].astype(F32)
            out[i] = total
            return 0

        lax.fori_loop(self.start, self.start + self.size, body, 0)

    def drain(self):
        for k in range(7):
            self.copy(k).wait_send()


def kernel(
    v_hbm, g_hbm, c_hbm, f1_hbm, f2_hbm,
    dv_hbm, dg_hbm, o1_hbm, o2_hbm,
    val, gate, up, f1, f2_own, f2_a, f2_b, f2_near, gated, back, sendb, ret, mix, mov, movt,
    part1, got1, part2n, got2n, part2c, got2c, part2d, got2d, out1, out2n, out2c, out2d, out2,
    lsem, osem, g2as, g2ar, g2bs, g2br, g2ns, g2nr, g1as, g1ar, g1bs, g1br,
    s1as, s1ar, s1bs, s1br, s2ns, s2nr, s2cs, s2cr, s2ds, s2dr, bs, br, ms, mr,
):
    at = Place()
    a, h = at.a, at.h
    z, xh, core = a // 4, (a // 2) % 2, a % 2
    pair0 = a // 2

    loads = []

    def load(src, dst):
        cp = pltpu.make_async_copy(src, dst, lsem.at[len(loads)])
        cp.start()
        loads.append(cp)
        return cp

    f2_in = load(f2_hbm, f2_own)
    f1_in = load(f1_hbm, f1.at[h])
    rest = []
    for s in range(2):
        lanes = pl.ds(128 * s, 128)
        rest.append(load(c_hbm.at[s], up.at[:, lanes]))
        rest.append(load(v_hbm.at[s], val.at[:, lanes]))
        rest.append(load(g_hbm.at[s], gate.at[:, lanes]))

    barrier = pltpu.get_barrier_semaphore()

    def greet(k, _):
        pl.semaphore_signal(barrier, inc=1, device_id=(lax.rem(a + k, N_CTX), h), device_id_type=MESH)
        return 0

    for d in range(1, N_CH):
        pl.semaphore_signal(barrier, inc=1, device_id=(a, at.piece(d // 2, d % 2)), device_id_type=MESH)
    lax.fori_loop(1, N_CTX, greet, 0)
    far_a = Direct(at, f2_a, None, g2as, g2ar)
    far_b = Direct(at, f2_b, None, g2bs, g2br)
    near = Gather(at, f2_near, g2ns, g2nr)
    one_a = Gather(at, f1, g1as, g1ar, 0, 4)
    one_b = Gather(at, f1, g1bs, g1br, 4, 4)

    f2_in.wait()
    turn = lax.rem(256 - 32 * lax.rem(z + 3, 8), 256)

    def turn_block(k, _):
        x = pltpu.roll(f2_own[2 * k].astype(F32), turn, 1)
        y = pltpu.roll(f2_own[2 * k + 1].astype(F32), turn, 1)
        f2_a[h, k] = jnp.concatenate([x[:, :64], y[:, :64]], axis=1).astype(BF16)
        f2_b[h, k] = jnp.concatenate([x[:, 64:128], y[:, 64:128]], axis=1).astype(BF16)
        f2_near[h, 2 * k] = x[:, 128:].astype(BF16)
        f2_near[h, 2 * k + 1] = y[:, 128:].astype(BF16)
        return 0

    lax.fori_loop(0, 8, turn_block, 0)
    pl.semaphore_wait(barrier, N_CTX - 1 + N_CH - 1)
    far_a.send()
    for cp in rest:
        cp.wait()

    def multiply(k, _):
        rows = pl.ds(pl.multiple_of(k * 512, 512), 512)
        gated[k] = (val[rows, :].astype(F32) * gate[rows, :].astype(F32)).astype(BF16)
        return 0

    lax.fori_loop(0, 8, multiply, 0)
    far_b.send()

    r = lax.broadcasted_iota(jnp.int32, (256, 256), 0)
    c = lax.broadcasted_iota(jnp.int32, (256, 256), 1)
    swap = jnp.where(((r >> 4) == (c & 15)) & ((r & 15) == (c >> 4)), 1.0, 0.0).astype(BF16)

    def back_copy(dst, src):
        row = lax.rem(src // 4 - dst // 4 + 14, 8) * 64 + lax.rem(src, 4) * 16
        return remote(sendb.at[dst], ret.at[:, pl.ds(pl.multiple_of(row, 16), 16), :], bs.at[dst], br.at[src], (dst, h))

    def upstream(k):
        return up[pl.ds(pl.multiple_of(k * 256, 256), 256), :]

    def back_send(first, row0, count):
        def send(k, _):
            xt = lax.rem(xh + k, 2)
            p = lax.rem(z + first + k // 2, 8) * 2 + xt
            row = pl.multiple_of(row0 + (k // 2) * 32 + xt * 16, 16)
            x = back[:, pl.ds(row, 16), :].reshape(256, 256)
            t = dot(swap, x, ((1,), (0,))).astype(BF16).reshape(2, 8, 16, 256)
            sendb[2 * p] = t[0]
            sendb[2 * p + 1] = t[1]

            @pl.when(p != pair0)
            def _():
                back_copy(2 * p + core, a).start()

            back_copy(2 * p + 1 - core, a).start()
            return 0

        lax.fori_loop(0, count, send, 0, unroll=2)

    def back_quarter(w_ref, first, row0):
        def block(k, _):
            w = w_ref[:, k].reshape(256, 128)
            back[2 * k, row0:row0 + 64] = dot(w[:, :64], upstream(2 * k), ((0,), (0,))).astype(BF16)
            back[2 * k + 1, row0:row0 + 64] = dot(w[:, 64:], upstream(2 * k + 1), ((0,), (0,))).astype(BF16)
            return 0

        lax.fori_loop(0, 8, block, 0, unroll=2)
        back_send(first, row0, 4)

    def back_near(k, _):
        back[k, 128:] = dot(f2_near[:, k].reshape(256, 128), upstream(k), ((0,), (0,))).astype(BF16)
        return 0

    far_a.wait()
    near.send(0, 1, 2)
    f1_in.wait()
    one_a.send(0, 1, 2)
    back_quarter(f2_a, 3, 0)
    far_b.wait()
    back_quarter(f2_b, 5, 64)
    near.wait(0)
    near.send(3, 4)
    one_a.wait(0)
    one_a.send(3, 4)
    near.wait(1)
    near.send(5)
    one_b.send(0, 1, 2)
    near.wait(4)
    near.send(6)
    one_a.wait(1)
    one_a.send(5)
    one_b.wait(0)
    one_b.send(3, 4)
    one_a.wait(4)
    one_a.send(6)
    one_b.wait(1)
    one_b.send(5)
    near.wait(2, 3, 5, 6)
    lax.fori_loop(0, 16, back_near, 0, unroll=4)
    back_send(7, 128, 8)
    ret[:, pl.ds(pl.multiple_of(384 + lax.rem(a, 4) * 16, 16), 16), :] = sendb[a]
    one_b.wait(4)
    one_b.send(6)

    def mix_block(i, _):
        mix[i] = dot(f1[:, i].reshape(512, 512), gated[i], ((1,), (0,))).astype(BF16)
        return 0

    def mix_copy(c, dst, slot):
        rows = pl.ds(pl.multiple_of(16 * dst, 16), 16)
        blocks = pl.ds(4 * c, 4)
        return remote(mix.at[blocks, rows, :], mov.at[slot, blocks], ms.at[c, dst], mr.at[c, slot], (dst, h))

    def mix_send(c, first, count):
        def send(k, _):
            p = lax.rem(z + first + k // 2, 8) * 2 + lax.rem(xh + k, 2)

            @pl.when(p != pair0)
            def _():
                mix_copy(c, 2 * p + core, a).start()

            mix_copy(c, 2 * p + 1 - core, a).start()
            return 0

        lax.fori_loop(0, count, send, 0)

    one_a.wait(2, 3, 5, 6)
    lax.fori_loop(0, 4, mix_block, 0, unroll=2)
    mix_send(0, 6, 12)

    def back_wait(k, _):
        src = lax.rem(a + k, N_CTX)
        back_copy(a, src).wait_recv()
        return 0

    lax.fori_loop(1, N_CTX, back_wait, 0)

    def grad_one_block(i, _):
        t = dot(ret[i], gated[i], ((1,), (1,))).astype(BF16).reshape(8, 64, 512)
        for q in range(8):
            part1[lax.rem(z + 2 + q, 8), i] = t[q]
        return 0

    def grad_input_block(i, _):
        w = jnp.concatenate([f1[lax.rem(z + 2 + q, 8), i] for q in range(8)], axis=0)
        grad = dot(w, ret[i], ((0,), (0,)))
        rows = pl.ds(pl.multiple_of(i * 512, 512), 512)
        v, g = val[rows, :].astype(F32), gate[rows, :].astype(F32)
        val[rows, :] = (grad * g).astype(BF16)
        gate[rows, :] = (grad * v).astype(BF16)
        return 0

    rs1a = Scatter(at, part1, got1, s1as, s1ar, 0, 4)
    rs1b = Scatter(at, part1, got1, s1bs, s1br, 4, 4)
    lax.fori_loop(0, 4, grad_one_block, 0, unroll=2)
    rs1a.first()
    one_b.wait(2, 3, 5, 6)
    lax.fori_loop(4, 8, mix_block, 0, unroll=2)
    mix_send(1, 6, 12)
    mov[a] = mix[:, pl.ds(pl.multiple_of(16 * a, 16), 16), :]
    lax.fori_loop(4, 8, grad_one_block, 0, unroll=2)
    rs1b.first()
    lax.fori_loop(0, 8, grad_input_block, 0, unroll=2)
    mix_send(0, 4, 4)
    mix_send(1, 4, 4)
    rs1a.second()
    stores = []

    def store(src, dst):
        cp = pltpu.make_async_copy(src, dst, osem.at[len(stores)])
        cp.start()
        stores.append(cp)

    for s in range(2):
        lanes = pl.ds(128 * s, 128)
        store(val.at[:, lanes], dv_hbm.at[s])
        store(gate.at[:, lanes], dg_hbm.at[s])

    def take(last, row0, count):
        def body(k, _):
            xt = lax.rem(xh + k, 2)
            p = lax.rem(z + last + 8 - k // 2, 8) * 2 + xt

            @pl.when(p != pair0)
            def _():
                mix_copy(0, 2 * p + core, 2 * p + core).wait_recv()
                mix_copy(1, 2 * p + core, 2 * p + core).wait_recv()

            mix_copy(0, 2 * p + 1 - core, 2 * p + 1 - core).wait_recv()
            mix_copy(1, 2 * p + 1 - core, 2 * p + 1 - core).wait_recv()
            x = mov[pl.ds(2 * p, 2)].reshape(256, 256)
            t = dot(swap, x, ((1,), (0,))).astype(BF16).reshape(16, 16, 256)
            row = pl.multiple_of(row0 - (k // 2) * 32 + xt * 16, 16)
            movt[:, pl.ds(row, 16), :] = t
            return 0

        lax.fori_loop(0, count, body, 0, unroll=2)

    def grad_two_near(k, _):
        t = dot(upstream(k), movt[k, 128:], ((1,), (1,))).astype(BF16)
        part2n[:, k] = t.reshape(8, 32, 128)
        return 0

    def grad_two_quarter(part, row0):
        def body(k, _):
            t = [dot(upstream(2 * k + e), movt[2 * k + e, row0:row0 + 64], ((1,), (1,))) for e in range(2)]
            part[:, k] = jnp.concatenate(t, axis=1).astype(BF16).reshape(8, 32, 128)
            return 0

        lax.fori_loop(0, 8, body, 0, unroll=2)

    rs2n = Scatter(at, part2n, got2n, s2ns, s2nr)
    rs2c = Scatter(at, part2c, got2c, s2cs, s2cr)
    rs2d = Direct(at, part2d, got2d, s2ds, s2dr)
    take(10, 224, 8)
    lax.fori_loop(0, 16, grad_two_near, 0, unroll=4)
    rs2n.first()
    rs1a.third()
    take(6, 96, 4)
    grad_two_quarter(part2c, 64)
    rs2c.first()
    rs1b.second()
    rs2n.second()
    rs2c.second()
    take(4, 32, 4)
    grad_two_quarter(part2d, 0)
    rs2d.send()
    rs1b.third()
    rs2n.third()
    rs2c.third()
    rs1a.last(out1)
    rs1b.last(out1)
    store(out1, o1_hbm)
    rs2n.last(out2n)
    rs2c.last(out2c)
    rs2d.last(out2d)
    unturn = 32 * lax.rem(z + 3, 8)

    def unturn_block(k, _):
        for e in range(2):
            lanes = slice(64 * e, 64 * e + 64)
            x = jnp.concatenate([out2d[k, :, lanes], out2c[k, :, lanes], out2n[2 * k + e]], axis=1)
            out2[2 * k + e] = pltpu.roll(x, unturn, 1)
        return 0

    lax.fori_loop(0, 8, unturn_block, 0)
    store(out2, o2_hbm)

    def drain(k, _):
        dst = lax.rem(a + k, N_CTX)
        back_copy(dst, a).wait_send()
        mix_copy(0, dst, a).wait_send()
        mix_copy(1, dst, a).wait_send()
        return 0

    lax.fori_loop(1, N_CTX, drain, 0)
    for x in (far_a, far_b, near, one_a, one_b, rs1a, rs1b, rs2n, rs2c, rs2d):
        x.drain()
    for cp in stores:
        cp.wait()


def per_device(values, gate, cotangent, factor_one, factor_two):
    vm = pltpu.VMEM
    dma = pltpu.SemaphoreType.DMA
    shapes = (
        jax.ShapeDtypeStruct(values.shape, BF16),
        jax.ShapeDtypeStruct(values.shape, BF16),
        jax.ShapeDtypeStruct(factor_one.shape, F32),
        jax.ShapeDtypeStruct(factor_two.shape, F32),
    )
    scratch = [
        vm((4096, 256), BF16), vm((4096, 256), BF16), vm((4096, 256), BF16),
        vm((8, 8, 64, 512), BF16),
        vm((16, 32, 256), BF16), vm((8, 8, 32, 128), BF16), vm((8, 8, 32, 128), BF16), vm((8, 16, 32, 128), BF16),
        vm((8, 512, 256), BF16),
        vm((16, 256, 256), BF16),
        vm((32, 8, 16, 256), BF16),
        vm((8, 512, 256), BF16),
        vm((8, 512, 256), BF16),
        vm((32, 8, 16, 256), BF16),
        vm((16, 256, 256), BF16),
        vm((8, 8, 64, 512), BF16), vm((7, 8, 64, 512), BF16),
        vm((8, 16, 32, 128), BF16), vm((7, 16, 32, 128), BF16),
        vm((8, 8, 32, 128), BF16), vm((7, 8, 32, 128), BF16),
        vm((8, 8, 32, 128), BF16), vm((7, 8, 32, 128), BF16),
        vm((8, 64, 512), F32),
        vm((16, 32, 128), F32), vm((8, 32, 128), F32), vm((8, 32, 128), F32), vm((16, 32, 256), F32),
        dma((8,)), dma((6,)),
        *[dma((7,)) for _ in range(20)],
        dma((32,)), dma((32,)), dma((2, 32)), dma((2, 32)),
    ]
    anywhere = pl.BlockSpec(memory_space=pl.ANY)
    return pl.pallas_call(
        kernel,
        out_shape=shapes,
        in_specs=[anywhere] * 5,
        out_specs=(anywhere,) * 4,
        scratch_shapes=scratch,
        compiler_params=pltpu.CompilerParams(
            collective_id=0, has_side_effects=True, vmem_limit_bytes=46 * 1024 * 1024
        ),
        name="monarch_backward",
    )(values, gate, cotangent, factor_one, factor_two)


def solution(mesh):
    tokens = P(None, "ctx", "ch")
    rows = P("ctx", "ch", None)
    return jax.shard_map(
        per_device,
        mesh=mesh,
        in_specs=(tokens, tokens, tokens, rows, rows),
        out_specs=(tokens, tokens, rows, rows),
        check_vma=False,
    )
```

```python
import jax
import jax.numpy as jnp
from jax import lax
from jax.experimental import pallas as pl
from jax.experimental.pallas import tpu as pltpu
from jax.sharding import PartitionSpec as P

MESH = pl.DeviceIdType.MESH
F32, BF16 = jnp.float32, jnp.bfloat16
N_CTX, N_CH = 32, 8
PAIRS = N_CTX // 2


def dot(a, b, dims):
    return lax.dot_general(a, b, (dims, ((), ())), preferred_element_type=F32)


class Place:
    def __init__(self):
        self.a = lax.axis_index("ctx")
        self.h = lax.axis_index("ch")
        self.y, self.xl = self.h // 2, self.h % 2
        self.xp = (self.a, self.piece(0, 1))
        self.yp = (self.a, self.piece(1, 0))
        self.ym = (self.a, self.piece(3, 0))

    def piece(self, dy, dx):
        xl = 1 - self.xl if dx else self.xl
        return lax.rem(self.y + dy, 4) * 2 + xl


def remote(src, dst, ssem, rsem, dev):
    return pltpu.make_async_remote_copy(
        src_ref=src, dst_ref=dst, send_sem=ssem, recv_sem=rsem, device_id=dev, device_id_type=MESH
    )


class Gather:
    def __init__(self, at, buf, ssem, rsem, start=0, size=None):
        self.at, self.buf, self.ssem, self.rsem = at, buf, ssem, rsem
        self.blocks = pl.ds(start, buf.shape[1] if size is None else size)
        p = at.piece
        self.plan = (
            (p(0, 0), at.xp, p(0, 1)),
            (p(0, 0), at.yp, p(3, 0)),
            (p(0, 0), at.ym, p(1, 0)),
            (p(0, 1), at.yp, p(3, 1)),
            (p(0, 1), at.ym, p(1, 1)),
            (p(3, 0), at.yp, p(2, 0)),
            (p(1, 1), at.ym, p(2, 1)),
        )

    def copy(self, k, arrives=False):
        sent, dev, came = self.plan[k]
        ref = self.buf.at[came if arrives else sent, self.blocks]
        return remote(ref, ref, self.ssem.at[k], self.rsem.at[k], dev)

    def send(self, *ks):
        for k in ks:
            self.copy(k).start()

    def wait(self, *ks):
        for k in ks:
            self.copy(k, True).wait_recv()

    def relay(self):
        self.wait(0)
        self.send(3, 4)
        self.wait(1)
        self.send(5)
        self.wait(4)
        self.send(6)

    def drain(self):
        for k in range(7):
            self.copy(k).wait_send()


class Direct:
    ORDER = (1, 4, 5, 2, 6, 3, 7)

    def __init__(self, at, part, got, ssem, rsem):
        self.at, self.part, self.got, self.ssem, self.rsem = at, part, got, ssem, rsem

    def copy(self, d):
        there = self.at.piece(d // 2, d % 2)
        if self.got is None:
            mine = self.part.at[self.at.piece(0, 0)]
            return remote(mine, mine, self.ssem.at[d - 1], self.rsem.at[d - 1], (self.at.a, there))
        return remote(self.part.at[there], self.got.at[d - 1], self.ssem.at[d - 1], self.rsem.at[d - 1], (self.at.a, there))

    def send(self):
        for d in self.ORDER:
            self.copy(d).start()

    def wait(self):
        for d in self.ORDER:
            if self.got is None:
                came = self.part.at[self.at.piece((8 - d // 2) % 4, d % 2)]
                remote(came, came, self.ssem.at[d - 1], self.rsem.at[d - 1], self.at.xp).wait_recv()
            else:
                self.copy(d).wait_recv()

    def last(self, out):
        self.wait()
        mine = self.at.piece(0, 0)

        def body(i, _):
            total = self.part[mine, i].astype(F32)
            for k in range(7):
                total += self.got[k, i].astype(F32)
            out[i] = total
            return 0

        lax.fori_loop(0, self.part.shape[1], body, 0, unroll=4)

    def drain(self):
        for d in self.ORDER:
            self.copy(d).wait_send()


class Scatter:
    def __init__(self, at, part, got, ssem, rsem, start=0, size=None):
        self.at, self.part, self.got, self.ssem, self.rsem = at, part, got, ssem, rsem
        self.start, self.size = start, part.shape[1] if size is None else size
        self.blocks = pl.ds(self.start, self.size)
        p = at.piece
        self.plan = (
            (p(2, 0), at.yp),
            (p(2, 1), at.ym),
            (p(1, 0), at.yp),
            (p(1, 1), at.yp),
            (p(3, 1), at.ym),
            (p(3, 0), at.ym),
            (p(0, 1), at.xp),
        )

    def copy(self, k):
        sent, dev = self.plan[k]
        return remote(
            self.part.at[sent, self.blocks], self.got.at[k, self.blocks], self.ssem.at[k], self.rsem.at[k], dev
        )

    def send(self, *ks):
        for k in ks:
            self.copy(k).start()

    def wait(self, *ks):
        for k in ks:
            self.copy(k).wait_recv()

    def add(self, piece, *ks):
        def body(i, _):
            total = self.part[piece, i].astype(F32)
            for k in ks:
                total += self.got[k, i].astype(F32)
            self.part[piece, i] = total.astype(BF16)
            return 0

        lax.fori_loop(self.start, self.start + self.size, body, 0, unroll=4)

    def first(self):
        self.send(0, 1, 3, 5)

    def second(self):
        self.wait(1)
        self.add(self.plan[4][0], 1)
        self.send(4)
        self.wait(0)
        self.add(self.plan[2][0], 0)
        self.send(2)

    def third(self):
        self.wait(3, 4)
        self.add(self.plan[6][0], 3, 4)
        self.send(6)

    def last(self, out):
        self.wait(2, 5, 6)
        mine = self.at.piece(0, 0)

        def body(i, _):
            total = self.part[mine, i].astype(F32)
            for k in (2, 5, 6):
                total += self.got[k, i].astype(F32)
            out[i] = total
            return 0

        lax.fori_loop(self.start, self.start + self.size, body, 0, unroll=4)

    def drain(self):
        for k in range(7):
            self.copy(k).wait_send()


def kernel(
    v_hbm, g_hbm, c_hbm, f1_hbm, f2_hbm,
    dv_hbm, dg_hbm, o1_hbm, o2_hbm,
    val, gate, up, f1, f2_own, f2_a, f2_b, f2_near, gated, back, sendb, ret, mix, mov, movt,
    part1, got1, part2n, got2n, part2c, got2c, part2d, got2d, out1, out2n, out2c, out2d, out2,
    lsem, osem, g2as, g2ar, g2bs, g2br, g2ns, g2nr, g1as, g1ar, g1bs, g1br,
    s1as, s1ar, s1bs, s1br, s2ns, s2nr, s2cs, s2cr, s2ds, s2dr, bs, br, ms, mr,
):
    at = Place()
    a, h = at.a, at.h
    z, xh, core = a // 4, (a // 2) % 2, a % 2
    pair0 = a // 2

    loads = []

    def load(src, dst):
        cp = pltpu.make_async_copy(src, dst, lsem.at[len(loads)])
        cp.start()
        loads.append(cp)
        return cp

    f2_in = load(f2_hbm, f2_own)
    f1_in = load(f1_hbm, f1.at[h])
    rest = []
    for s in range(2):
        lanes = pl.ds(128 * s, 128)
        rest.append(load(c_hbm.at[s], up.at[:, lanes]))
        rest.append(load(v_hbm.at[s], val.at[:, lanes]))
        rest.append(load(g_hbm.at[s], gate.at[:, lanes]))

    barrier = pltpu.get_barrier_semaphore()

    def greet(k, _):
        pl.semaphore_signal(barrier, inc=1, device_id=(lax.rem(a + k, N_CTX), h), device_id_type=MESH)
        return 0

    for d in range(1, N_CH):
        pl.semaphore_signal(barrier, inc=1, device_id=(a, at.piece(d // 2, d % 2)), device_id_type=MESH)
    lax.fori_loop(1, N_CTX, greet, 0)
    far_a = Direct(at, f2_a, None, g2as, g2ar)
    far_b = Direct(at, f2_b, None, g2bs, g2br)
    near = Gather(at, f2_near, g2ns, g2nr)
    one_a = Gather(at, f1, g1as, g1ar, 0, 4)
    one_b = Gather(at, f1, g1bs, g1br, 4, 4)

    f2_in.wait()
    turn = lax.rem(256 - 32 * lax.rem(z + 3, 8), 256)

    def turn_block(k, _):
        x = pltpu.roll(f2_own[2 * k].astype(F32), turn, 1)
        y = pltpu.roll(f2_own[2 * k + 1].astype(F32), turn, 1)
        f2_a[h, k] = jnp.concatenate([x[:, :64], y[:, :64]], axis=1).astype(BF16)
        f2_b[h, k] = jnp.concatenate([x[:, 64:128], y[:, 64:128]], axis=1).astype(BF16)
        f2_near[h, 2 * k] = x[:, 128:].astype(BF16)
        f2_near[h, 2 * k + 1] = y[:, 128:].astype(BF16)
        return 0

    lax.fori_loop(0, 8, turn_block, 0, unroll=4)
    pl.semaphore_wait(barrier, N_CTX - 1 + N_CH - 1)
    far_a.send()
    for cp in rest:
        cp.wait()

    def multiply(k, _):
        rows = pl.ds(pl.multiple_of(k * 512, 512), 512)
        gated[k] = (val[rows, :].astype(F32) * gate[rows, :].astype(F32)).astype(BF16)
        return 0

    lax.fori_loop(0, 8, multiply, 0)
    far_b.send()

    r = lax.broadcasted_iota(jnp.int32, (256, 256), 0)
    c = lax.broadcasted_iota(jnp.int32, (256, 256), 1)
    swap = jnp.where(((r >> 4) == (c & 15)) & ((r & 15) == (c >> 4)), 1.0, 0.0).astype(BF16)

    def back_copy(dst, src):
        row = lax.rem(src // 4 - dst // 4 + 14, 8) * 64 + lax.rem(src, 4) * 16
        return remote(sendb.at[dst], ret.at[:, pl.ds(pl.multiple_of(row, 16), 16), :], bs.at[dst], br.at[src], (dst, h))

    def upstream(k):
        return up[pl.ds(pl.multiple_of(k * 256, 256), 256), :]

    def back_send(first, row0, count):
        def send(k, _):
            xt = lax.rem(xh + k, 2)
            p = lax.rem(z + first + k // 2, 8) * 2 + xt
            row = pl.multiple_of(row0 + (k // 2) * 32 + xt * 16, 16)
            x = back[:, pl.ds(row, 16), :].reshape(256, 256)
            t = dot(swap, x, ((1,), (0,))).astype(BF16).reshape(2, 8, 16, 256)
            sendb[2 * p] = t[0]
            sendb[2 * p + 1] = t[1]

            @pl.when(p != pair0)
            def _():
                back_copy(2 * p + core, a).start()

            back_copy(2 * p + 1 - core, a).start()
            return 0

        lax.fori_loop(0, count, send, 0, unroll=2)

    def back_quarter(w_ref, first, row0):
        def block(k, _):
            w = w_ref[:, k].reshape(256, 128)
            back[2 * k, row0:row0 + 64] = dot(w[:, :64], upstream(2 * k), ((0,), (0,))).astype(BF16)
            back[2 * k + 1, row0:row0 + 64] = dot(w[:, 64:], upstream(2 * k + 1), ((0,), (0,))).astype(BF16)
            return 0

        lax.fori_loop(0, 8, block, 0, unroll=2)
        back_send(first, row0, 4)

    def back_near(k, _):
        back[k, 128:] = dot(f2_near[:, k].reshape(256, 128), upstream(k), ((0,), (0,))).astype(BF16)
        return 0

    far_a.wait()
    near.send(0, 1, 2)
    f1_in.wait()
    one_a.send(0, 1, 2)
    back_quarter(f2_a, 3, 0)
    far_b.wait()
    back_quarter(f2_b, 5, 64)
    near.wait(0)
    near.send(3, 4)
    one_a.wait(0)
    one_a.send(3, 4)
    near.wait(1)
    near.send(5)
    one_b.send(0, 1, 2)
    near.wait(4)
    near.send(6)
    one_a.wait(1)
    one_a.send(5)
    one_b.wait(0)
    one_b.send(3, 4)
    one_a.wait(4)
    one_a.send(6)
    one_b.wait(1)
    one_b.send(5)
    near.wait(2, 3, 5, 6)
    lax.fori_loop(0, 16, back_near, 0, unroll=4)
    back_send(7, 128, 8)
    ret[:, pl.ds(pl.multiple_of(384 + lax.rem(a, 4) * 16, 16), 16), :] = sendb[a]
    one_b.wait(4)
    one_b.send(6)

    def mix_block(i, _):
        mix[i] = dot(f1[:, i].reshape(512, 512), gated[i], ((1,), (0,))).astype(BF16)
        return 0

    def mix_copy(c, dst, slot):
        rows = pl.ds(pl.multiple_of(16 * dst, 16), 16)
        blocks = pl.ds(4 * c, 4)
        return remote(mix.at[blocks, rows, :], mov.at[slot, blocks], ms.at[c, dst], mr.at[c, slot], (dst, h))

    def mix_send(c, first, count):
        def send(k, _):
            p = lax.rem(z + first + k // 2, 8) * 2 + lax.rem(xh + k, 2)

            @pl.when(p != pair0)
            def _():
                mix_copy(c, 2 * p + core, a).start()

            mix_copy(c, 2 * p + 1 - core, a).start()
            return 0

        lax.fori_loop(0, count, send, 0)

    one_a.wait(2, 3, 5, 6)
    lax.fori_loop(0, 4, mix_block, 0, unroll=2)
    mix_send(0, 6, 12)

    def back_wait(k, _):
        src = lax.rem(a + k, N_CTX)
        back_copy(a, src).wait_recv()
        return 0

    lax.fori_loop(1, N_CTX, back_wait, 0)

    def grad_one_block(i, _):
        t = dot(ret[i], gated[i], ((1,), (1,))).astype(BF16).reshape(8, 64, 512)
        for q in range(8):
            part1[lax.rem(z + 2 + q, 8), i] = t[q]
        return 0

    def grad_input_block(i, _):
        w = jnp.concatenate([f1[lax.rem(z + 2 + q, 8), i] for q in range(8)], axis=0)
        grad = dot(w, ret[i], ((0,), (0,)))
        rows = pl.ds(pl.multiple_of(i * 512, 512), 512)
        v, g = val[rows, :].astype(F32), gate[rows, :].astype(F32)
        val[rows, :] = (grad * g).astype(BF16)
        gate[rows, :] = (grad * v).astype(BF16)
        return 0

    rs1a = Scatter(at, part1, got1, s1as, s1ar, 0, 4)
    rs1b = Scatter(at, part1, got1, s1bs, s1br, 4, 4)
    lax.fori_loop(0, 4, grad_one_block, 0, unroll=2)
    rs1a.first()
    one_b.wait(2, 3, 5, 6)
    lax.fori_loop(4, 8, mix_block, 0, unroll=2)
    mix_send(1, 6, 12)
    mov[a] = mix[:, pl.ds(pl.multiple_of(16 * a, 16), 16), :]
    lax.fori_loop(4, 8, grad_one_block, 0, unroll=2)
    rs1b.first()
    lax.fori_loop(0, 8, grad_input_block, 0, unroll=2)
    mix_send(0, 4, 4)
    mix_send(1, 4, 4)
    rs1a.second()
    stores = []

    def store(src, dst):
        cp = pltpu.make_async_copy(src, dst, osem.at[len(stores)])
        cp.start()
        stores.append(cp)

    for s in range(2):
        lanes = pl.ds(128 * s, 128)
        store(val.at[:, lanes], dv_hbm.at[s])
        store(gate.at[:, lanes], dg_hbm.at[s])

    def take(last, row0, count):
        def body(k, _):
            xt = lax.rem(xh + k, 2)
            p = lax.rem(z + last + 8 - k // 2, 8) * 2 + xt

            @pl.when(p != pair0)
            def _():
                mix_copy(0, 2 * p + core, 2 * p + core).wait_recv()
                mix_copy(1, 2 * p + core, 2 * p + core).wait_recv()

            mix_copy(0, 2 * p + 1 - core, 2 * p + 1 - core).wait_recv()
            mix_copy(1, 2 * p + 1 - core, 2 * p + 1 - core).wait_recv()
            x = mov[pl.ds(2 * p, 2)].reshape(256, 256)
            t = dot(swap, x, ((1,), (0,))).astype(BF16).reshape(16, 16, 256)
            row = pl.multiple_of(row0 - (k // 2) * 32 + xt * 16, 16)
            movt[:, pl.ds(row, 16), :] = t
            return 0

        lax.fori_loop(0, count, body, 0, unroll=2)

    def grad_two_near(k, _):
        t = dot(upstream(k), movt[k, 128:], ((1,), (1,))).astype(BF16)
        part2n[:, k] = t.reshape(8, 32, 128)
        return 0

    def grad_two_quarter(part, row0):
        def body(k, _):
            t = [dot(upstream(2 * k + e), movt[2 * k + e, row0:row0 + 64], ((1,), (1,))) for e in range(2)]
            part[:, k] = jnp.concatenate(t, axis=1).astype(BF16).reshape(8, 32, 128)
            return 0

        lax.fori_loop(0, 8, body, 0, unroll=2)

    rs2n = Scatter(at, part2n, got2n, s2ns, s2nr)
    rs2c = Scatter(at, part2c, got2c, s2cs, s2cr)
    rs2d = Direct(at, part2d, got2d, s2ds, s2dr)
    take(10, 224, 8)
    lax.fori_loop(0, 16, grad_two_near, 0, unroll=4)
    rs2n.first()
    rs1a.third()
    take(6, 96, 4)
    grad_two_quarter(part2c, 64)
    rs2c.first()
    rs1b.second()
    rs2n.second()
    rs2c.second()
    take(4, 32, 4)
    grad_two_quarter(part2d, 0)
    rs2d.send()
    rs1b.third()
    rs2n.third()
    rs2c.third()
    rs1a.last(out1)
    rs1b.last(out1)
    store(out1, o1_hbm)
    rs2n.last(out2n)
    rs2c.last(out2c)
    rs2d.last(out2d)
    unturn = 32 * lax.rem(z + 3, 8)

    def unturn_block(k, _):
        for e in range(2):
            lanes = slice(64 * e, 64 * e + 64)
            x = jnp.concatenate([out2d[k, :, lanes], out2c[k, :, lanes], out2n[2 * k + e]], axis=1)
            out2[2 * k + e] = pltpu.roll(x, unturn, 1)
        return 0

    lax.fori_loop(0, 8, unturn_block, 0, unroll=4)
    store(out2, o2_hbm)

    def drain(k, _):
        dst = lax.rem(a + k, N_CTX)
        back_copy(dst, a).wait_send()
        mix_copy(0, dst, a).wait_send()
        mix_copy(1, dst, a).wait_send()
        return 0

    lax.fori_loop(1, N_CTX, drain, 0)
    for x in (far_a, far_b, near, one_a, one_b, rs1a, rs1b, rs2n, rs2c, rs2d):
        x.drain()
    for cp in stores:
        cp.wait()


def per_device(values, gate, cotangent, factor_one, factor_two):
    vm = pltpu.VMEM
    dma = pltpu.SemaphoreType.DMA
    shapes = (
        jax.ShapeDtypeStruct(values.shape, BF16),
        jax.ShapeDtypeStruct(values.shape, BF16),
        jax.ShapeDtypeStruct(factor_one.shape, F32),
        jax.ShapeDtypeStruct(factor_two.shape, F32),
    )
    scratch = [
        vm((4096, 256), BF16), vm((4096, 256), BF16), vm((4096, 256), BF16),
        vm((8, 8, 64, 512), BF16),
        vm((16, 32, 256), BF16), vm((8, 8, 32, 128), BF16), vm((8, 8, 32, 128), BF16), vm((8, 16, 32, 128), BF16),
        vm((8, 512, 256), BF16),
        vm((16, 256, 256), BF16),
        vm((32, 8, 16, 256), BF16),
        vm((8, 512, 256), BF16),
        vm((8, 512, 256), BF16),
        vm((32, 8, 16, 256), BF16),
        vm((16, 256, 256), BF16),
        vm((8, 8, 64, 512), BF16), vm((7, 8, 64, 512), BF16),
        vm((8, 16, 32, 128), BF16), vm((7, 16, 32, 128), BF16),
        vm((8, 8, 32, 128), BF16), vm((7, 8, 32, 128), BF16),
        vm((8, 8, 32, 128), BF16), vm((7, 8, 32, 128), BF16),
        vm((8, 64, 512), F32),
        vm((16, 32, 128), F32), vm((8, 32, 128), F32), vm((8, 32, 128), F32), vm((16, 32, 256), F32),
        dma((8,)), dma((6,)),
        *[dma((7,)) for _ in range(20)],
        dma((32,)), dma((32,)), dma((2, 32)), dma((2, 32)),
    ]
    anywhere = pl.BlockSpec(memory_space=pl.ANY)
    return pl.pallas_call(
        kernel,
        out_shape=shapes,
        in_specs=[anywhere] * 5,
        out_specs=(anywhere,) * 4,
        scratch_shapes=scratch,
        compiler_params=pltpu.CompilerParams(
            collective_id=0, has_side_effects=True, vmem_limit_bytes=46 * 1024 * 1024
        ),
        name="monarch_backward",
    )(values, gate, cotangent, factor_one, factor_two)


def solution(mesh):
    tokens = P(None, "ctx", "ch")
    rows = P("ctx", "ch", None)
    return jax.shard_map(
        per_device,
        mesh=mesh,
        in_specs=(tokens, tokens, tokens, rows, rows),
        out_specs=(tokens, tokens, rows, rows),
        check_vma=False,
    )
```
